32 devices in a mesh: front: 4 (over z), row: 4 (over x, core), col: 2 (over y).
Axes of the slice: x: 2, y: 2, z: 4, core: 2. Of those that a mesh axis runs over, the one named last changes fastest.
Arguments:
- sigma_anc: bfloat16 [8192, 8192], P(('front', 'row'), 'col'), may hold values from -6 to 6
- update_blocks: int32 [4, 32], replicated, may hold values from 0 to 63, as said below
- panel: bfloat16 [4, 4096, 2048], P('front', 'col'), may hold values from -0.09375 to 0.09375
Outputs:
- sigma_ju: bfloat16 [4, 2048, 4096], P('front', 'col', 'row')
The draws below stay inside these ranges and needn't reach their ends.
Inputs may be any that keep to these rules, and one draw needn't show every extreme that they name: `update_blocks`: A front's update blocks are 32 distinct blocks in increasing order along the row. Each class of blocks g, (g // 4) mod (4), holds exactly 8 of them, and each aligned run of 32 blocks holds exactly 16 of them.
All inputs are finite; a program needn't handle non-finite values.
Results may differ from the reference program's by a relative error of at most 0.017.
Values may be sent and summed in bfloat16 or wider, within the bound.
A program may use at most 64 MiB of HBM per device.

```python
import jax
import jax.numpy as jnp
from jax import lax

BLK = 128
NANC = 4
SEPB = 16
UB = 32
SJ = 2048
FRONTS = 4
AN = 8192
U = 4096
RBL = 4
OCT = 16
N_FRONT = 4
N_ROW = 4
N_COL = 2


def class_order(pair_key):
    return jax.random.permutation(pair_key, N_ROW).astype(jnp.int32)


def update_picks(key):
    blocks_total = NANC * SEPB
    octant_size = blocks_total // N_COL
    cell_size = blocks_total // (N_COL * N_ROW)
    half_cell = cell_size // 2
    range_size = blocks_total // (N_FRONT * N_ROW)
    positions = jnp.arange(blocks_total, dtype=jnp.int32)
    cell_of = positions // octant_size * N_ROW + positions // range_size % N_ROW

    def one_front(front_key):
        keys = jax.random.split(front_key, 4)
        octant_order = jax.random.permutation(keys[0], N_COL).astype(jnp.int32)
        class_pairs = jax.vmap(class_order)(jax.random.split(keys[1], N_COL // 2))
        shifts = jax.random.randint(keys[2], (N_COL // 2,), 0, half_cell + 1).astype(jnp.int32)
        first_octant = octant_order[0::2]
        second_octant = octant_order[1::2]
        class_one = class_pairs[:, 0]
        class_two = class_pairs[:, 1]
        counts = jnp.full((N_COL, N_ROW), half_cell, jnp.int32)
        counts = counts.at[first_octant, class_one].add(shifts)
        counts = counts.at[first_octant, class_two].add(-shifts)
        counts = counts.at[second_octant, class_one].add(-shifts)
        counts = counts.at[second_octant, class_two].add(shifts)
        scrambled = jax.random.permutation(keys[3], blocks_total).astype(jnp.int32)
        ordering = jnp.argsort(cell_of * blocks_total + scrambled)
        rank_sorted = positions - jnp.take(cell_of, ordering) * cell_size
        ranks = jnp.zeros(blocks_total, jnp.int32).at[ordering].set(rank_sorted)
        chosen = ranks < jnp.take(counts.reshape(-1), cell_of)
        picked = jnp.argsort(jnp.where(chosen, positions, positions + blocks_total))[:UB]
        return picked.astype(jnp.int32)
    return jax.vmap(one_front)(jax.random.split(key, FRONTS))


def draw_update_blocks(key, part):
    return update_picks(jax.random.fold_in(key, 11)).astype(jnp.int32)


def steps_of(rng, extent, pieces, low, high):
    factor_of, own = 1.0, jax.random.fold_in(rng, 6)
    for axis_at, parts in pieces:
        heights = jnp.exp(jax.random.uniform(jax.random.fold_in(own, axis_at), (parts,), jnp.float32, low / len(pieces), high / len(pieces)))
        factor_of = factor_of * jnp.repeat(heights, extent[axis_at] // parts).reshape([-1 if axis == axis_at else 1 for axis in range(len(extent))])
    return factor_of


def bell_draw(rng, extent, deviation, reach, shards=(), kind=jnp.bfloat16):
    level = steps_of(rng, extent, shards, -0.22, 0.18) if shards else 1.0
    entries = jax.random.normal(rng, extent, jnp.float32) * deviation * level
    return jnp.minimum(jnp.maximum(entries, -reach), reach).astype(kind)


def setup_inputs(seed: int = 0) -> dict:
    key_list = jax.random.split(jax.random.key(seed), 4)
    sigma_anc = bell_draw(key_list[0], (AN, AN), 1.0, 6.0, ((0, 16), (1, 2)))
    update_blocks = draw_update_blocks(jax.random.fold_in(key_list[3], 71), 0)
    panel = bell_draw(key_list[2], (FRONTS, U, SJ), U ** -0.5, 0.09375, ((0, 4), (1, 2)))
    return {"sigma_anc": sigma_anc, "update_blocks": update_blocks, "panel": panel}


def reference(sigma_anc, update_blocks, panel):
    blocks_total = NANC * SEPB
    blocked = sigma_anc.reshape(blocks_total, BLK, blocks_total, BLK)
    run_rows = OCT * BLK

    def one_front(inputs):
        block_ids, panel_front = inputs
        picked = block_ids.astype(jnp.int32)
        classes = (picked // RBL) % N_ROW
        ordering = jnp.argsort(classes * UB + jnp.arange(UB, dtype=jnp.int32))
        listed = jnp.take(picked, ordering)
        row_pick = jnp.take(blocked, listed, axis=0)
        square = jnp.take(row_pick, picked, axis=2).reshape(UB * BLK, UB * BLK)
        accumulated = jnp.zeros((UB * BLK, SJ), jnp.float32)
        for octant in range(UB // OCT):
            col_slice = square[:, octant * run_rows:(octant + 1) * run_rows]
            panel_slice = panel_front[octant * run_rows:(octant + 1) * run_rows]
            partial_value = jnp.dot(col_slice, panel_slice, preferred_element_type=jnp.float32)
            rounded = lax.optimization_barrier(partial_value.astype(jnp.bfloat16))
            accumulated = accumulated + rounded.astype(jnp.float32)
        return (-accumulated.T).astype(jnp.bfloat16)

    return lax.map(one_front, (update_blocks, panel))
```

```python
import functools

import jax
import jax.numpy as jnp
from jax import lax
from jax.experimental import pallas as pl
from jax.experimental.pallas import tpu as pltpu
from jax.sharding import PartitionSpec as P

BLK = 128
NANC = 4
SEPB = 16
UB = 32
MESH = pl.DeviceIdType.MESH


def flipped(index, mask, count):
    total, bit = 0, 1
    while bit < count:
        digit = lax.rem(lax.div(index, bit), 2)
        total = total + (1 - digit if mask & bit else digit) * bit
        bit *= 2
    return total


def kernel(
    fronts, rows, cols,
    chosen_ref, panel_ref, result,
    panel, inbox, part, landed,
    own_sem, panel_sem, send_sem, recv_sem, part_send, part_recv,
):
    my_front = lax.axis_index("front")
    my_col = lax.axis_index("col")
    slots = chosen_ref.shape[1]
    wide = panel_ref.shape[1]
    share = wide // cols
    tile = min(512, share)
    per_share = share // tile
    masks = list(range(fronts - 1, 0, -1))

    def own_copy(slot):
        return pltpu.make_async_copy(
            chosen_ref.at[my_front, slot], inbox.at[0, slot], own_sem.at[slot]
        )

    panel_copy = pltpu.make_async_copy(panel_ref, panel, panel_sem)

    barrier = pltpu.get_barrier_semaphore()
    for mask in masks:
        pl.semaphore_signal(
            barrier, inc=1, device_id={"front": flipped(my_front, mask, fronts)}, device_id_type=MESH
        )
    for step in range(1, cols):
        pl.semaphore_signal(
            barrier, inc=1, device_id={"col": lax.rem(my_col + step, cols)}, device_id_type=MESH
        )
    pl.semaphore_wait(barrier, fronts - 1 + cols - 1)

    def front_copy(mask, slot):
        return pltpu.make_async_remote_copy(
            src_ref=chosen_ref.at[flipped(my_front, mask, fronts), slot],
            dst_ref=inbox.at[mask, slot],
            send_sem=send_sem.at[mask - 1, slot],
            recv_sem=recv_sem.at[mask - 1, slot],
            device_id={"front": flipped(my_front, mask, fronts)},
            device_id_type=MESH,
        )

    def dispatch(slot, carry):
        for mask in masks:
            front_copy(mask, slot).start()
        return carry

    lax.fori_loop(0, slots, dispatch, 0)
    for slot in range(slots):
        own_copy(slot).start()
    panel_copy.start()
    for slot in range(slots):
        own_copy(slot).wait()
    panel_copy.wait()

    def part_copy(mask, slot, step):
        return pltpu.make_async_remote_copy(
            src_ref=part.at[mask, slot, lax.rem(my_col + step, cols)],
            dst_ref=landed.at[mask, slot, step - 1],
            send_sem=part_send.at[mask, slot, step - 1],
            recv_sem=part_recv.at[mask, slot, step - 1],
            device_id={"col": lax.rem(my_col + step, cols)},
            device_id_type=MESH,
        )

    def multiply(mask, slot):
        def one_tile(n, carry):
            lanes = pl.ds(pl.multiple_of(n * tile, tile), tile)
            inner = pl.ds(pl.multiple_of(lax.rem(n, per_share) * tile, tile), tile)
            product = jnp.dot(inbox[mask, slot], panel[:, lanes], preferred_element_type=jnp.float32)
            part[mask, slot, lax.div(n, per_share), :, inner] = product.astype(part.dtype)
            return carry

        lax.fori_loop(0, wide // tile, one_tile, 0)
        for step in range(1, cols):
            part_copy(mask, slot, step).start()

    def finish(mask, slot):
        for step in range(1, cols):
            part_copy(mask, slot, step).wait_recv()
        place = flipped(my_front, mask, fronts) * slots + slot
        width = min(256, share)
        for at in range(0, share, width):
            total = part[mask, slot, my_col, :, at:at + width].astype(jnp.float32)
            for step in range(1, cols):
                total = total + landed[mask, slot, step - 1, :, at:at + width].astype(jnp.float32)
            result[place, at:at + width, :] = (-total).T.astype(result.dtype)

    def own_product(slot, carry):
        multiply(0, slot)
        return carry

    lax.fori_loop(0, slots, own_product, 0)

    def own_finish(slot, carry):
        finish(0, slot)
        return carry

    lax.fori_loop(0, slots, own_finish, 0)

    def arrival(slot, carry):
        for mask in range(1, fronts):
            front_copy(mask, slot).wait_recv()
            multiply(mask, slot)
            if mask > 1:
                finish(mask - 1, slot)
            else:
                @pl.when(slot > 0)
                def _():
                    finish(fronts - 1, slot - 1)
        return carry

    lax.fori_loop(0, slots, arrival, 0)

    finish(fronts - 1, slots - 1)

    def drain(slot, carry):
        for mask in range(fronts):
            if mask > 0:
                front_copy(mask, slot).wait_send()
            for step in range(1, cols):
                part_copy(mask, slot, step).wait_send()
        return carry

    lax.fori_loop(0, slots, drain, 0)


def choose(cols, ids_ref, sigma_ref, chosen_ref):
    my_col = lax.axis_index("col")
    octant_blocks = NANC * SEPB // cols
    picks = UB // cols
    for front in range(chosen_ref.shape[0]):
        for j in range(picks):
            column = ids_ref[front, my_col * picks + j] - my_col * octant_blocks
            lanes = pl.ds(pl.multiple_of(column * BLK, BLK), BLK)
            chosen_ref[front, 0, :, j * BLK:(j + 1) * BLK] = sigma_ref[:, lanes]


def arrange(slots, rows, ids_ref, result_ref, out_ref):
    my_front = lax.axis_index("front")
    my_row = lax.axis_index("row")
    class_picks = UB // rows
    count = jnp.int32(0)
    places = [jnp.int32(0)] * class_picks
    for i in range(UB):
        block = ids_ref[my_front, i]
        hit = lax.rem(lax.div(block, slots), rows) == my_row
        place = lax.div(block, slots * rows) * slots + lax.rem(block, slots)
        for k in range(min(class_picks, i + 1)):
            places[k] = jnp.where(jnp.logical_and(hit, count == k), place, places[k])
        count = count + jnp.where(hit, 1, 0)
    for k, place in enumerate(places):
        out_ref[:, k * BLK:(k + 1) * BLK] = result_ref[place]


def solution(mesh):
    fronts, rows, cols = mesh.shape["front"], mesh.shape["row"], mesh.shape["col"]

    def on_device(sigma_anc, update_blocks, panel):
        depth, wide = panel.shape[1:]
        share = wide // cols
        slots = sigma_anc.shape[0] // BLK
        kind = sigma_anc.dtype
        smem = pl.BlockSpec(memory_space=pltpu.SMEM)
        vmem = pl.BlockSpec(memory_space=pltpu.VMEM)
        hbm = pl.BlockSpec(memory_space=pl.ANY)
        chosen = pl.pallas_call(
            functools.partial(choose, cols),
            grid=(slots,),
            out_shape=jax.ShapeDtypeStruct((fronts, slots, BLK, depth), kind),
            in_specs=[smem, pl.BlockSpec((BLK, sigma_anc.shape[1]), lambda slot: (slot, 0))],
            out_specs=pl.BlockSpec((fronts, 1, BLK, depth), lambda slot: (0, slot, 0, 0)),
            compiler_params=pltpu.CompilerParams(vmem_limit_bytes=32 * 1024 * 1024),
        )(update_blocks, sigma_anc)
        result = pl.pallas_call(
            functools.partial(kernel, fronts, rows, cols),
            out_shape=jax.ShapeDtypeStruct((fronts * slots, share, BLK), kind),
            in_specs=[hbm, hbm],
            out_specs=vmem,
            scratch_shapes=[
                pltpu.VMEM((depth, wide), kind),
                pltpu.VMEM((fronts, slots, BLK, depth), kind),
                pltpu.VMEM((fronts, slots, cols, BLK, share), kind),
                pltpu.VMEM((fronts, slots, cols - 1, BLK, share), kind),
                pltpu.SemaphoreType.DMA((slots,)),
                pltpu.SemaphoreType.DMA,
                pltpu.SemaphoreType.DMA((fronts - 1, slots)),
                pltpu.SemaphoreType.DMA((fronts - 1, slots)),
                pltpu.SemaphoreType.DMA((fronts, slots, cols - 1)),
                pltpu.SemaphoreType.DMA((fronts, slots, cols - 1)),
            ],
            compiler_params=pltpu.CompilerParams(
                collective_id=0, has_side_effects=True, vmem_limit_bytes=56 * 1024 * 1024
            ),
            cost_estimate=pl.CostEstimate(
                flops=2 * fronts * slots * BLK * depth * wide,
                bytes_accessed=2 * (sigma_anc.size + panel[0].size),
                transcendentals=0,
            ),
        )(chosen, panel[0])
        product = pl.pallas_call(
            functools.partial(arrange, slots, rows),
            out_shape=jax.ShapeDtypeStruct((share, UB // rows * BLK), kind),
            in_specs=[smem, vmem],
            out_specs=vmem,
            compiler_params=pltpu.CompilerParams(vmem_limit_bytes=32 * 1024 * 1024),
        )(update_blocks, result)
        return product[None]

    placed = (P(("front", "row"), "col"), P(), P("front", "col", None))
    return jax.shard_map(
        on_device, mesh=mesh, in_specs=placed, out_specs=P("front", "col", "row"), check_vma=False
    )
```

```python
import functools

import jax
import jax.numpy as jnp
from jax import lax
from jax.experimental import pallas as pl
from jax.experimental.pallas import tpu as pltpu
from jax.sharding import PartitionSpec as P

BLK = 128
NANC = 4
SEPB = 16
UB = 32
MESH = pl.DeviceIdType.MESH


def flipped(index, mask, count):
    total, bit = 0, 1
    while bit < count:
        digit = lax.rem(lax.div(index, bit), 2)
        total = total + (1 - digit if mask & bit else digit) * bit
        bit *= 2
    return total


def deal(fronts, rows, sigma_ref, dealt_ref, own_sem, send_sem, recv_sem):
    my_front = lax.axis_index("front")
    my_row = lax.axis_index("row")
    strip = BLK // (2 * rows)
    side = lax.rem(my_front, 2)
    place = side * rows + my_row

    def strips(to_side, to_row):
        return sigma_ref.at[:, pl.ds(pl.multiple_of((to_row * 2 + to_side) * strip, strip), strip)]

    moves = [(flip, step) for flip in (1, 0) for step in range(rows) if flip or step]

    def target(flip, step):
        return {
            "front": flipped(my_front, flip, fronts),
            "row": lax.rem(my_row + step, rows),
        }

    own = pltpu.make_async_copy(strips(side, my_row), dealt_ref.at[place], own_sem)
    own.start()
    barrier = pltpu.get_barrier_semaphore()
    for flip, step in moves:
        pl.semaphore_signal(barrier, inc=1, device_id=target(flip, step), device_id_type=MESH)
    pl.semaphore_wait(barrier, len(moves))
    copies = []
    for flip, step in moves:
        to_side = 1 - side if flip else side
        copies.append(
            pltpu.make_async_remote_copy(
                src_ref=strips(to_side, lax.rem(my_row + step, rows)),
                dst_ref=dealt_ref.at[place],
                send_sem=send_sem.at[flip, step],
                recv_sem=recv_sem.at[flip, step],
                device_id=target(flip, step),
                device_id_type=MESH,
            )
        )
    for copy in copies:
        copy.start()
    own.wait()
    for copy in copies:
        copy.wait()


def choose(cols, ids_ref, dealt_ref, chosen_ref):
    front = pl.program_id(0)
    octant = lax.div(lax.axis_index("front"), 2)
    my_col = lax.axis_index("col")
    octant_blocks = NANC * SEPB // cols
    picks = UB // cols
    pieces = chosen_ref.shape[1]
    strip = dealt_ref.shape[1]
    each = picks // pieces
    lanes = []
    for j in range(picks):
        column = ids_ref[front, my_col * picks + j] - my_col * octant_blocks
        lanes.append(pl.ds(pl.multiple_of(column * BLK, BLK), BLK))
    for p in range(picks):
        block = ids_ref[front, octant * picks + p] - octant * octant_blocks
        at = p % each * strip
        for j in range(picks):
            chosen_ref[0, p // each, at:at + strip, j * BLK:(j + 1) * BLK] = dealt_ref[block, :, lanes[j]]


def kernel(
    fronts, rows, cols,
    chosen_ref, panel_ref, result,
    panel, inbox, part, landed,
    own_sem, panel_sem, send_sem, recv_sem, part_send, part_recv, row_send, row_recv,
):
    my_front = lax.axis_index("front")
    my_row = lax.axis_index("row")
    my_col = lax.axis_index("col")
    pieces = chosen_ref.shape[1]
    strip = BLK // (2 * rows)
    picks = UB // cols
    each = picks // pieces
    wide = panel_ref.shape[1]
    share = wide // cols
    tile = min(512, share)
    per_share = share // tile
    masks = list(range(fronts - 1, 0, -1))

    def own_copy(piece):
        return pltpu.make_async_copy(
            chosen_ref.at[my_front, piece], inbox.at[0, piece], own_sem.at[piece]
        )

    panel_copy = pltpu.make_async_copy(panel_ref, panel, panel_sem)

    barrier = pltpu.get_barrier_semaphore()
    for mask in masks:
        pl.semaphore_signal(
            barrier, inc=1, device_id={"front": flipped(my_front, mask, fronts)}, device_id_type=MESH
        )
    for step in range(1, cols):
        pl.semaphore_signal(
            barrier, inc=1, device_id={"col": lax.rem(my_col + step, cols)}, device_id_type=MESH
        )
    for step in range(1, rows):
        pl.semaphore_signal(
            barrier, inc=1, device_id={"row": lax.rem(my_row + step, rows)}, device_id_type=MESH
        )
    pl.semaphore_wait(barrier, fronts + cols + rows - 3)

    def front_copy(mask, piece):
        return pltpu.make_async_remote_copy(
            src_ref=chosen_ref.at[flipped(my_front, mask, fronts), piece],
            dst_ref=inbox.at[mask, piece],
            send_sem=send_sem.at[mask - 1, piece],
            recv_sem=recv_sem.at[mask - 1, piece],
            device_id={"front": flipped(my_front, mask, fronts)},
            device_id_type=MESH,
        )

    def dispatch(piece, carry):
        for mask in masks:
            front_copy(mask, piece).start()
        return carry

    lax.fori_loop(0, pieces, dispatch, 0)
    for piece in range(pieces):
        own_copy(piece).start()
    panel_copy.start()
    for piece in range(pieces):
        own_copy(piece).wait()
    panel_copy.wait()

    def part_copy(mask, piece, step):
        return pltpu.make_async_remote_copy(
            src_ref=part.at[mask, piece, lax.rem(my_col + step, cols)],
            dst_ref=landed.at[mask, piece, step - 1],
            send_sem=part_send.at[mask, piece, step - 1],
            recv_sem=part_recv.at[mask, piece, step - 1],
            device_id={"col": lax.rem(my_col + step, cols)},
            device_id_type=MESH,
        )

    def spot(mask, piece):
        source = flipped(my_front, mask, fronts)
        first = lax.div(source, 2) * picks + piece * each
        offset = (my_row * 2 + lax.rem(source, 2)) * strip
        return first, pl.ds(pl.multiple_of(offset, strip), strip)

    def row_copy(mask, piece, step):
        first, lines = spot(mask, piece)
        return pltpu.make_async_remote_copy(
            src_ref=result.at[pl.ds(first, each), lines],
            dst_ref=result.at[pl.ds(first, each), lines],
            send_sem=row_send.at[mask, piece, step - 1],
            recv_sem=row_recv.at[mask, piece, step - 1],
            device_id={"row": lax.rem(my_row + step, rows)},
            device_id_type=MESH,
        )

    def multiply(mask, piece):
        def one_tile(n, carry):
            lanes = pl.ds(pl.multiple_of(n * tile, tile), tile)
            inner = pl.ds(pl.multiple_of(lax.rem(n, per_share) * tile, tile), tile)
            product = jnp.dot(inbox[mask, piece], panel[:, lanes], preferred_element_type=jnp.float32)
            part[mask, piece, lax.div(n, per_share), :, inner] = product.astype(part.dtype)
            return carry

        lax.fori_loop(0, wide // tile, one_tile, 0)
        for step in range(1, cols):
            part_copy(mask, piece, step).start()

    def finish(mask, piece):
        for step in range(1, cols):
            part_copy(mask, piece, step).wait_recv()
        first, lines = spot(mask, piece)
        for p in range(each):
            inside = slice(p * strip, (p + 1) * strip)
            total = part[mask, piece, my_col, inside, :].astype(jnp.float32)
            for step in range(1, cols):
                total = total + landed[mask, piece, step - 1, inside, :].astype(jnp.float32)
            result[first + p, lines, :] = (-total).astype(result.dtype)
        for step in range(1, rows):
            row_copy(mask, piece, step).start()

    for mask in (0, 1):
        def product_of(piece, carry, mask=mask):
            if mask:
                front_copy(mask, piece).wait_recv()
            multiply(mask, piece)
            return carry

        def total_of(piece, carry, mask=mask):
            finish(mask, piece)
            return carry

        lax.fori_loop(0, pieces, product_of, 0)
        lax.fori_loop(0, pieces, total_of, 0)

    def arrival(piece, carry):
        for mask in range(2, fronts):
            front_copy(mask, piece).wait_recv()
            multiply(mask, piece)
            if mask > 2:
                finish(mask - 1, piece)
            else:
                @pl.when(piece > 0)
                def _():
                    finish(fronts - 1, piece - 1)
        return carry

    lax.fori_loop(0, pieces, arrival, 0)
    finish(fronts - 1, pieces - 1)

    def drain(piece, carry):
        for mask in range(fronts):
            if mask > 0:
                front_copy(mask, piece).wait_send()
            for step in range(1, cols):
                part_copy(mask, piece, step).wait_send()
            for step in range(1, rows):
                row_copy(mask, piece, step).wait()
        return carry

    lax.fori_loop(0, pieces, drain, 0)


def arrange(slots, rows, ids_ref, result_ref, out_ref):
    my_front = lax.axis_index("front")
    my_row = lax.axis_index("row")
    class_picks = UB // rows
    count = jnp.int32(0)
    places = [jnp.int32(0)] * class_picks
    for i in range(UB):
        hit = lax.rem(lax.div(ids_ref[my_front, i], slots), rows) == my_row
        for k in range(min(class_picks, i + 1)):
            places[k] = jnp.where(jnp.logical_and(hit, count == k), i, places[k])
        count = count + jnp.where(hit, 1, 0)
    for k, place in enumerate(places):
        out_ref[:, k * BLK:(k + 1) * BLK] = result_ref[place].T


def solution(mesh):
    fronts, rows, cols = mesh.shape["front"], mesh.shape["row"], mesh.shape["col"]

    def on_device(sigma_anc, update_blocks, panel):
        depth, wide = panel.shape[1:]
        share = wide // cols
        slots = sigma_anc.shape[0] // BLK
        across = sigma_anc.shape[1]
        kind = sigma_anc.dtype
        strip = BLK // (2 * rows)
        picks = UB // cols
        pieces = min(4, picks)
        lines = picks // pieces * strip
        smem = pl.BlockSpec(memory_space=pltpu.SMEM)
        vmem = pl.BlockSpec(memory_space=pltpu.VMEM)
        hbm = pl.BlockSpec(memory_space=pl.ANY)
        mib = 1024 * 1024
        dealt = pl.pallas_call(
            functools.partial(deal, fronts, rows),
            out_shape=jax.ShapeDtypeStruct((2 * rows, slots, strip, across), kind),
            in_specs=[hbm],
            out_specs=hbm,
            scratch_shapes=[
                pltpu.SemaphoreType.DMA,
                pltpu.SemaphoreType.DMA((2, rows)),
                pltpu.SemaphoreType.DMA((2, rows)),
            ],
            compiler_params=pltpu.CompilerParams(
                collective_id=1, has_side_effects=True, vmem_limit_bytes=56 * mib
            ),
        )(sigma_anc.reshape(slots, BLK, across))
        chosen = pl.pallas_call(
            functools.partial(choose, cols),
            grid=(fronts,),
            out_shape=jax.ShapeDtypeStruct((fronts, pieces, lines, depth), kind),
            in_specs=[smem, vmem],
            out_specs=pl.BlockSpec((1, pieces, lines, depth), lambda front: (front, 0, 0, 0)),
            compiler_params=pltpu.CompilerParams(vmem_limit_bytes=56 * mib),
        )(update_blocks, dealt.reshape(2 * rows * slots, strip, across))
        result = pl.pallas_call(
            functools.partial(kernel, fronts, rows, cols),
            out_shape=jax.ShapeDtypeStruct((UB, BLK, share), kind),
            in_specs=[hbm, hbm],
            out_specs=vmem,
            scratch_shapes=[
                pltpu.VMEM((depth, wide), kind),
                pltpu.VMEM((fronts, pieces, lines, depth), kind),
                pltpu.VMEM((fronts, pieces, cols, lines, share), kind),
                pltpu.VMEM((fronts, pieces, cols - 1, lines, share), kind),
                pltpu.SemaphoreType.DMA((pieces,)),
                pltpu.SemaphoreType.DMA,
                pltpu.SemaphoreType.DMA((fronts - 1, pieces)),
                pltpu.SemaphoreType.DMA((fronts - 1, pieces)),
                pltpu.SemaphoreType.DMA((fronts, pieces, cols - 1)),
                pltpu.SemaphoreType.DMA((fronts, pieces, cols - 1)),
                pltpu.SemaphoreType.DMA((fronts, pieces, rows - 1)),
                pltpu.SemaphoreType.DMA((fronts, pieces, rows - 1)),
            ],
            compiler_params=pltpu.CompilerParams(
                collective_id=0, has_side_effects=True, vmem_limit_bytes=56 * mib
            ),
            cost_estimate=pl.CostEstimate(
                flops=2 * fronts * pieces * lines * depth * wide,
                bytes_accessed=2 * (sigma_anc.size + panel[0].size),
                transcendentals=0,
            ),
        )(chosen, panel[0])
        product = pl.pallas_call(
            functools.partial(arrange, slots, rows),
            out_shape=jax.ShapeDtypeStruct((share, UB // rows * BLK), kind),
            in_specs=[smem, vmem],
            out_specs=vmem,
            compiler_params=pltpu.CompilerParams(vmem_limit_bytes=56 * mib),
        )(update_blocks, result)
        return product[None]

    placed = (P(("front", "row"), "col"), P(), P("front", "col", None))
    return jax.shard_map(
        on_device, mesh=mesh, in_specs=placed, out_specs=P("front", "col", "row"), check_vma=False
    )
```

```python
import functools

import jax
import jax.numpy as jnp
from jax import lax
from jax.experimental import pallas as pl
from jax.experimental.pallas import tpu as pltpu
from jax.sharding import PartitionSpec as P

BLK = 128
NANC = 4
SEPB = 16
UB = 32
MESH = pl.DeviceIdType.MESH


def flipped(index, mask, count):
    total, bit = 0, 1
    while bit < count:
        digit = lax.rem(lax.div(index, bit), 2)
        total = total + (1 - digit if mask & bit else digit) * bit
        bit *= 2
    return total


def deal(fronts, rows, sigma_ref, dealt_ref, own_sem, send_sem, recv_sem):
    my_front = lax.axis_index("front")
    my_row = lax.axis_index("row")
    strip = BLK // (2 * rows)
    side = lax.rem(my_front, 2)
    place = side * rows + my_row

    def strips(to_side, to_row):
        return sigma_ref.at[:, pl.ds(pl.multiple_of((to_row * 2 + to_side) * strip, strip), strip)]

    moves = [(flip, step) for flip in (1, 0) for step in range(rows) if flip or step]

    def target(flip, step):
        return {
            "front": flipped(my_front, flip, fronts),
            "row": lax.rem(my_row + step, rows),
        }

    own = pltpu.make_async_copy(strips(side, my_row), dealt_ref.at[place], own_sem)
    own.start()
    barrier = pltpu.get_barrier_semaphore()
    for flip, step in moves:
        pl.semaphore_signal(barrier, inc=1, device_id=target(flip, step), device_id_type=MESH)
    pl.semaphore_wait(barrier, len(moves))
    copies = []
    for flip, step in moves:
        to_side = 1 - side if flip else side
        copies.append(
            pltpu.make_async_remote_copy(
                src_ref=strips(to_side, lax.rem(my_row + step, rows)),
                dst_ref=dealt_ref.at[place],
                send_sem=send_sem.at[flip, step],
                recv_sem=recv_sem.at[flip, step],
                device_id=target(flip, step),
                device_id_type=MESH,
            )
        )
    for copy in copies:
        copy.start()
    own.wait()
    for copy in copies:
        copy.wait()


def choose(cols, ids_ref, dealt_ref, chosen_ref):
    front = pl.program_id(0)
    octant = lax.div(lax.axis_index("front"), 2)
    my_col = lax.axis_index("col")
    octant_blocks = NANC * SEPB // cols
    picks = UB // cols
    pieces = chosen_ref.shape[1]
    strip = dealt_ref.shape[1]
    each = picks // pieces
    lanes = []
    for j in range(picks):
        column = ids_ref[front, my_col * picks + j] - my_col * octant_blocks
        lanes.append(pl.ds(pl.multiple_of(column * BLK, BLK), BLK))
    for p in range(picks):
        block = ids_ref[front, octant * picks + p] - octant * octant_blocks
        at = p % each * strip
        for j in range(picks):
            chosen_ref[0, p // each, at:at + strip, j * BLK:(j + 1) * BLK] = dealt_ref[block, :, lanes[j]]


def kernel(
    fronts, rows, cols,
    chosen_ref, panel_ref, result,
    panel, inbox, part, landed,
    own_sem, panel_sem, send_sem, recv_sem, part_send, part_recv, row_send, row_recv,
):
    my_front = lax.axis_index("front")
    my_row = lax.axis_index("row")
    my_col = lax.axis_index("col")
    pieces = chosen_ref.shape[1]
    strip = BLK // (2 * rows)
    picks = UB // cols
    each = picks // pieces
    wide = panel_ref.shape[1]
    share = wide // cols
    tile = min(512, share)
    per_share = share // tile
    masks = list(range(fronts - 1, 0, -1))
    order = masks[::-1]

    def own_copy(piece):
        return pltpu.make_async_copy(
            chosen_ref.at[my_front, piece], inbox.at[0, piece], own_sem.at[piece]
        )

    panel_copy = pltpu.make_async_copy(panel_ref, panel, panel_sem)

    barrier = pltpu.get_barrier_semaphore()
    for mask in masks:
        pl.semaphore_signal(
            barrier, inc=1, device_id={"front": flipped(my_front, mask, fronts)}, device_id_type=MESH
        )
    for step in range(1, cols):
        pl.semaphore_signal(
            barrier, inc=1, device_id={"col": lax.rem(my_col + step, cols)}, device_id_type=MESH
        )
    for step in range(1, rows):
        pl.semaphore_signal(
            barrier, inc=1, device_id={"row": lax.rem(my_row + step, rows)}, device_id_type=MESH
        )
    pl.semaphore_wait(barrier, fronts + cols + rows - 3)

    def front_copy(mask, piece):
        return pltpu.make_async_remote_copy(
            src_ref=chosen_ref.at[flipped(my_front, mask, fronts), piece],
            dst_ref=inbox.at[mask, piece],
            send_sem=send_sem.at[mask - 1, piece],
            recv_sem=recv_sem.at[mask - 1, piece],
            device_id={"front": flipped(my_front, mask, fronts)},
            device_id_type=MESH,
        )

    def dispatch(piece, carry):
        for mask in masks:
            front_copy(mask, piece).start()
        return carry

    lax.fori_loop(0, pieces, dispatch, 0)
    for piece in range(pieces):
        own_copy(piece).start()
    panel_copy.start()
    for piece in range(pieces):
        own_copy(piece).wait()
    panel_copy.wait()

    def part_copy(mask, piece, step):
        return pltpu.make_async_remote_copy(
            src_ref=part.at[mask, piece, lax.rem(my_col + step, cols)],
            dst_ref=landed.at[mask, piece, step - 1],
            send_sem=part_send.at[mask, piece, step - 1],
            recv_sem=part_recv.at[mask, piece, step - 1],
            device_id={"col": lax.rem(my_col + step, cols)},
            device_id_type=MESH,
        )

    def spot(mask, piece):
        source = flipped(my_front, mask, fronts)
        first = lax.div(source, 2) * picks + piece * each
        offset = (my_row * 2 + lax.rem(source, 2)) * strip
        return first, pl.ds(pl.multiple_of(offset, strip), strip)

    def row_copy(mask, piece, step):
        first, lines = spot(mask, piece)
        return pltpu.make_async_remote_copy(
            src_ref=result.at[pl.ds(first, each), lines],
            dst_ref=result.at[pl.ds(first, each), lines],
            send_sem=row_send.at[mask, piece, step - 1],
            recv_sem=row_recv.at[mask, piece, step - 1],
            device_id={"row": lax.rem(my_row + step, rows)},
            device_id_type=MESH,
        )

    def multiply(mask, piece):
        def one_tile(n, carry):
            lanes = pl.ds(pl.multiple_of(n * tile, tile), tile)
            inner = pl.ds(pl.multiple_of(lax.rem(n, per_share) * tile, tile), tile)
            product = jnp.dot(inbox[mask, piece], panel[:, lanes], preferred_element_type=jnp.float32)
            part[mask, piece, lax.div(n, per_share), :, inner] = product.astype(part.dtype)
            return carry

        lax.fori_loop(0, wide // tile, one_tile, 0)
        for step in range(1, cols):
            part_copy(mask, piece, step).start()

    def finish(mask, piece):
        for step in range(1, cols):
            part_copy(mask, piece, step).wait_recv()
        first, lines = spot(mask, piece)
        for p in range(each):
            inside = slice(p * strip, (p + 1) * strip)
            total = part[mask, piece, my_col, inside, :].astype(jnp.float32)
            for step in range(1, cols):
                total = total + landed[mask, piece, step - 1, inside, :].astype(jnp.float32)
            result[first + p, lines, :] = (-total).astype(result.dtype)
        for step in range(1, rows):
            row_copy(mask, piece, step).start()

    def own_product(piece, carry):
        multiply(0, piece)
        return carry

    def own_total(piece, carry):
        finish(0, piece)
        return carry

    lax.fori_loop(0, pieces, own_product, 0)
    lax.fori_loop(0, pieces, own_total, 0)

    def arrival(piece, carry):
        for at, mask in enumerate(order):
            front_copy(mask, piece).wait_recv()
            multiply(mask, piece)
            if at:
                finish(order[at - 1], piece)
            else:
                @pl.when(piece > 0)
                def _():
                    finish(order[-1], piece - 1)
        return carry

    lax.fori_loop(0, pieces, arrival, 0)
    finish(order[-1], pieces - 1)

    def drain(piece, carry):
        for mask in range(fronts):
            if mask > 0:
                front_copy(mask, piece).wait_send()
            for step in range(1, cols):
                part_copy(mask, piece, step).wait_send()
            for step in range(1, rows):
                row_copy(mask, piece, step).wait()
        return carry

    lax.fori_loop(0, pieces, drain, 0)


def arrange(slots, rows, ids_ref, result_ref, out_ref):
    my_front = lax.axis_index("front")
    my_row = lax.axis_index("row")
    class_picks = UB // rows
    count = jnp.int32(0)
    places = [jnp.int32(0)] * class_picks
    for i in range(UB):
        hit = lax.rem(lax.div(ids_ref[my_front, i], slots), rows) == my_row
        for k in range(min(class_picks, i + 1)):
            places[k] = jnp.where(jnp.logical_and(hit, count == k), i, places[k])
        count = count + jnp.where(hit, 1, 0)
    for k, place in enumerate(places):
        out_ref[:, k * BLK:(k + 1) * BLK] = result_ref[place].T


def solution(mesh):
    fronts, rows, cols = mesh.shape["front"], mesh.shape["row"], mesh.shape["col"]

    def on_device(sigma_anc, update_blocks, panel):
        depth, wide = panel.shape[1:]
        share = wide // cols
        slots = sigma_anc.shape[0] // BLK
        across = sigma_anc.shape[1]
        kind = sigma_anc.dtype
        strip = BLK // (2 * rows)
        picks = UB // cols
        pieces = min(4, picks)
        lines = picks // pieces * strip
        smem = pl.BlockSpec(memory_space=pltpu.SMEM)
        vmem = pl.BlockSpec(memory_space=pltpu.VMEM)
        hbm = pl.BlockSpec(memory_space=pl.ANY)
        mib = 1024 * 1024
        dealt = pl.pallas_call(
            functools.partial(deal, fronts, rows),
            out_shape=jax.ShapeDtypeStruct((2 * rows, slots, strip, across), kind),
            in_specs=[hbm],
            out_specs=hbm,
            scratch_shapes=[
                pltpu.SemaphoreType.DMA,
                pltpu.SemaphoreType.DMA((2, rows)),
                pltpu.SemaphoreType.DMA((2, rows)),
            ],
            compiler_params=pltpu.CompilerParams(
                collective_id=1, has_side_effects=True, vmem_limit_bytes=56 * mib
            ),
        )(sigma_anc.reshape(slots, BLK, across))
        chosen = pl.pallas_call(
            functools.partial(choose, cols),
            grid=(fronts,),
            out_shape=jax.ShapeDtypeStruct((fronts, pieces, lines, depth), kind),
            in_specs=[smem, vmem],
            out_specs=pl.BlockSpec((1, pieces, lines, depth), lambda front: (front, 0, 0, 0)),
            compiler_params=pltpu.CompilerParams(vmem_limit_bytes=56 * mib),
        )(update_blocks, dealt.reshape(2 * rows * slots, strip, across))
        result = pl.pallas_call(
            functools.partial(kernel, fronts, rows, cols),
            out_shape=jax.ShapeDtypeStruct((UB, BLK, share), kind),
            in_specs=[hbm, hbm],
            out_specs=vmem,
            scratch_shapes=[
                pltpu.VMEM((depth, wide), kind),
                pltpu.VMEM((fronts, pieces, lines, depth), kind),
                pltpu.VMEM((fronts, pieces, cols, lines, share), kind),
                pltpu.VMEM((fronts, pieces, cols - 1, lines, share), kind),
                pltpu.SemaphoreType.DMA((pieces,)),
                pltpu.SemaphoreType.DMA,
                pltpu.SemaphoreType.DMA((fronts - 1, pieces)),
                pltpu.SemaphoreType.DMA((fronts - 1, pieces)),
                pltpu.SemaphoreType.DMA((fronts, pieces, cols - 1)),
                pltpu.SemaphoreType.DMA((fronts, pieces, cols - 1)),
                pltpu.SemaphoreType.DMA((fronts, pieces, rows - 1)),
                pltpu.SemaphoreType.DMA((fronts, pieces, rows - 1)),
            ],
            compiler_params=pltpu.CompilerParams(
                collective_id=0, has_side_effects=True, vmem_limit_bytes=56 * mib
            ),
            cost_estimate=pl.CostEstimate(
                flops=2 * fronts * pieces * lines * depth * wide,
                bytes_accessed=2 * (sigma_anc.size + panel[0].size),
                transcendentals=0,
            ),
        )(chosen, panel[0])
        product = pl.pallas_call(
            functools.partial(arrange, slots, rows),
            out_shape=jax.ShapeDtypeStruct((share, UB // rows * BLK), kind),
            in_specs=[smem, vmem],
            out_specs=vmem,
            compiler_params=pltpu.CompilerParams(vmem_limit_bytes=56 * mib),
        )(update_blocks, result)
        return product[None]

    placed = (P(("front", "row"), "col"), P(), P("front", "col", None))
    return jax.shard_map(
        on_device, mesh=mesh, in_specs=placed, out_specs=P("front", "col", "row"), check_vma=False
    )
```

```python
import functools

import jax
import jax.numpy as jnp
from jax import lax
from jax.experimental import pallas as pl
from jax.experimental.pallas import tpu as pltpu
from jax.sharding import PartitionSpec as P

BLK = 128
NANC = 4
SEPB = 16
UB = 32
MESH = pl.DeviceIdType.MESH


def flipped(index, mask, count):
    total, bit = 0, 1
    while bit < count:
        digit = lax.rem(lax.div(index, bit), 2)
        total = total + (1 - digit if mask & bit else digit) * bit
        bit *= 2
    return total


def deal(fronts, rows, sigma_ref, dealt_ref, own_sem, send_sem, recv_sem):
    my_front = lax.axis_index("front")
    my_row = lax.axis_index("row")
    strip = BLK // (2 * rows)
    side = lax.rem(my_front, 2)
    place = side * rows + my_row

    def strips(to_side, to_row):
        return sigma_ref.at[:, pl.ds(pl.multiple_of((to_row * 2 + to_side) * strip, strip), strip)]

    moves = [(flip, step) for flip in (1, 0) for step in range(rows) if flip or step]

    def target(flip, step):
        return {
            "front": flipped(my_front, flip, fronts),
            "row": lax.rem(my_row + step, rows),
        }

    own = pltpu.make_async_copy(strips(side, my_row), dealt_ref.at[place], own_sem)
    own.start()
    barrier = pltpu.get_barrier_semaphore()
    for flip, step in moves:
        pl.semaphore_signal(barrier, inc=1, device_id=target(flip, step), device_id_type=MESH)
    pl.semaphore_wait(barrier, len(moves))
    copies = []
    for flip, step in moves:
        to_side = 1 - side if flip else side
        copies.append(
            pltpu.make_async_remote_copy(
                src_ref=strips(to_side, lax.rem(my_row + step, rows)),
                dst_ref=dealt_ref.at[place],
                send_sem=send_sem.at[flip, step],
                recv_sem=recv_sem.at[flip, step],
                device_id=target(flip, step),
                device_id_type=MESH,
            )
        )
    for copy in copies:
        copy.start()
    own.wait()
    for copy in copies:
        copy.wait()


def choose(cols, ids_ref, dealt_ref, chosen_ref):
    front = pl.program_id(0)
    octant = lax.div(lax.axis_index("front"), 2)
    my_col = lax.axis_index("col")
    octant_blocks = NANC * SEPB // cols
    picks = UB // cols
    pieces = chosen_ref.shape[1]
    strip = dealt_ref.shape[1]
    each = picks // pieces
    lanes = []
    for j in range(picks):
        column = ids_ref[front, my_col * picks + j] - my_col * octant_blocks
        lanes.append(pl.ds(pl.multiple_of(column * BLK, BLK), BLK))
    for p in range(picks):
        block = ids_ref[front, octant * picks + p] - octant * octant_blocks
        at = p % each * strip
        for j in range(picks):
            chosen_ref[0, p // each, at:at + strip, j * BLK:(j + 1) * BLK] = dealt_ref[block, :, lanes[j]]


def kernel(
    fronts, rows, cols,
    chosen_ref, panel_ref, result,
    panel, inbox, part, landed,
    own_sem, panel_sem, send_sem, recv_sem, part_send, part_recv, row_send, row_recv,
):
    my_front = lax.axis_index("front")
    my_row = lax.axis_index("row")
    my_col = lax.axis_index("col")
    pieces = chosen_ref.shape[1]
    strip = BLK // (2 * rows)
    picks = UB // cols
    each = picks // pieces
    wide = panel_ref.shape[1]
    share = wide // cols
    tile = min(512, share)
    per_share = share // tile
    masks = list(range(fronts - 1, 0, -1))
    order = masks[::-1]

    def own_copy(piece):
        return pltpu.make_async_copy(
            chosen_ref.at[my_front, piece], inbox.at[0, piece], own_sem.at[piece]
        )

    panel_copy = pltpu.make_async_copy(panel_ref, panel, panel_sem)

    barrier = pltpu.get_barrier_semaphore()
    for mask in masks:
        pl.semaphore_signal(
            barrier, inc=1, device_id={"front": flipped(my_front, mask, fronts)}, device_id_type=MESH
        )
    for step in range(1, cols):
        pl.semaphore_signal(
            barrier, inc=1, device_id={"col": lax.rem(my_col + step, cols)}, device_id_type=MESH
        )
    for step in range(1, rows):
        pl.semaphore_signal(
            barrier, inc=1, device_id={"row": lax.rem(my_row + step, rows)}, device_id_type=MESH
        )
    pl.semaphore_wait(barrier, fronts + cols + rows - 3)

    def front_copy(mask, piece):
        return pltpu.make_async_remote_copy(
            src_ref=chosen_ref.at[flipped(my_front, mask, fronts), piece],
            dst_ref=inbox.at[mask, piece],
            send_sem=send_sem.at[mask - 1, piece],
            recv_sem=recv_sem.at[mask - 1, piece],
            device_id={"front": flipped(my_front, mask, fronts)},
            device_id_type=MESH,
        )

    def dispatch(piece, carry):
        for mask in masks:
            front_copy(mask, piece).start()
        return carry

    lax.fori_loop(0, pieces, dispatch, 0)
    for piece in range(pieces):
        own_copy(piece).start()
    panel_copy.start()
    for piece in range(pieces):
        own_copy(piece).wait()
    panel_copy.wait()

    def part_copy(mask, piece, step):
        return pltpu.make_async_remote_copy(
            src_ref=part.at[mask, piece, lax.rem(my_col + step, cols)],
            dst_ref=landed.at[mask, piece, step - 1],
            send_sem=part_send.at[mask, piece, step - 1],
            recv_sem=part_recv.at[mask, piece, step - 1],
            device_id={"col": lax.rem(my_col + step, cols)},
            device_id_type=MESH,
        )

    def spot(mask, piece, row):
        source = flipped(my_front, mask, fronts)
        first = lax.div(source, 2) * picks + piece * each
        offset = (row * 2 + lax.rem(source, 2)) * strip
        return first, pl.ds(pl.multiple_of(offset, strip), strip)

    def row_copy(mask, piece, kind):
        first, lines = spot(mask, piece, flipped(my_row, 2, rows) if kind == 2 else my_row)
        return pltpu.make_async_remote_copy(
            src_ref=result.at[pl.ds(first, each), lines],
            dst_ref=result.at[pl.ds(first, each), lines],
            send_sem=row_send.at[mask, piece, kind],
            recv_sem=row_recv.at[mask, piece, kind],
            device_id={"row": flipped(my_row, 1 if kind else 2, rows)},
            device_id_type=MESH,
        )

    def relay(mask, piece):
        row_copy(mask, piece, 0).wait_recv()
        row_copy(mask, piece, 2).start()

    def multiply(mask, piece):
        def one_tile(n, carry):
            lanes = pl.ds(pl.multiple_of(n * tile, tile), tile)
            inner = pl.ds(pl.multiple_of(lax.rem(n, per_share) * tile, tile), tile)
            product = jnp.dot(inbox[mask, piece], panel[:, lanes], preferred_element_type=jnp.float32)
            part[mask, piece, lax.div(n, per_share), :, inner] = product.astype(part.dtype)
            return carry

        lax.fori_loop(0, wide // tile, one_tile, 0)
        for step in range(1, cols):
            part_copy(mask, piece, step).start()

    def finish(mask, piece):
        for step in range(1, cols):
            part_copy(mask, piece, step).wait_recv()
        first, lines = spot(mask, piece, my_row)
        for p in range(each):
            inside = slice(p * strip, (p + 1) * strip)
            total = part[mask, piece, my_col, inside, :].astype(jnp.float32)
            for step in range(1, cols):
                total = total + landed[mask, piece, step - 1, inside, :].astype(jnp.float32)
            result[first + p, lines, :] = (-total).astype(result.dtype)
        row_copy(mask, piece, 0).start()
        row_copy(mask, piece, 1).start()

    def own_product(piece, carry):
        multiply(0, piece)
        return carry

    def own_total(piece, carry):
        finish(0, piece)
        return carry

    lax.fori_loop(0, pieces, own_product, 0)
    lax.fori_loop(0, pieces, own_total, 0)

    def own_relay(piece, carry):
        relay(0, piece)
        return carry

    lax.fori_loop(0, pieces, own_relay, 0)

    def arrival(piece, carry):
        for at, mask in enumerate(order):
            front_copy(mask, piece).wait_recv()
            multiply(mask, piece)
            for lag, action in ((1, finish), (2, relay)):
                if at >= lag:
                    action(order[at - lag], piece)
                else:
                    @pl.when(piece > 0)
                    def _(action=action, earlier=order[at - lag]):
                        action(earlier, piece - 1)
        return carry

    lax.fori_loop(0, pieces, arrival, 0)
    finish(order[-1], pieces - 1)
    relay(order[-2], pieces - 1)
    relay(order[-1], pieces - 1)

    def drain(piece, carry):
        for mask in range(fronts):
            if mask > 0:
                front_copy(mask, piece).wait_send()
            for step in range(1, cols):
                part_copy(mask, piece, step).wait_send()
            row_copy(mask, piece, 0).wait_send()
            row_copy(mask, piece, 1).wait()
            row_copy(mask, piece, 2).wait()
        return carry

    lax.fori_loop(0, pieces, drain, 0)


def arrange(slots, rows, ids_ref, result_ref, out_ref):
    my_front = lax.axis_index("front")
    my_row = lax.axis_index("row")
    class_picks = UB // rows
    count = jnp.int32(0)
    places = [jnp.int32(0)] * class_picks
    for i in range(UB):
        hit = lax.rem(lax.div(ids_ref[my_front, i], slots), rows) == my_row
        for k in range(min(class_picks, i + 1)):
            places[k] = jnp.where(jnp.logical_and(hit, count == k), i, places[k])
        count = count + jnp.where(hit, 1, 0)
    for k, place in enumerate(places):
        out_ref[:, k * BLK:(k + 1) * BLK] = result_ref[place].T


def solution(mesh):
    fronts, rows, cols = mesh.shape["front"], mesh.shape["row"], mesh.shape["col"]

    def on_device(sigma_anc, update_blocks, panel):
        depth, wide = panel.shape[1:]
        share = wide // cols
        slots = sigma_anc.shape[0] // BLK
        across = sigma_anc.shape[1]
        kind = sigma_anc.dtype
        strip = BLK // (2 * rows)
        picks = UB // cols
        pieces = min(4, picks)
        lines = picks // pieces * strip
        smem = pl.BlockSpec(memory_space=pltpu.SMEM)
        vmem = pl.BlockSpec(memory_space=pltpu.VMEM)
        hbm = pl.BlockSpec(memory_space=pl.ANY)
        mib = 1024 * 1024
        dealt = pl.pallas_call(
            functools.partial(deal, fronts, rows),
            out_shape=jax.ShapeDtypeStruct((2 * rows, slots, strip, across), kind),
            in_specs=[hbm],
            out_specs=hbm,
            scratch_shapes=[
                pltpu.SemaphoreType.DMA,
                pltpu.SemaphoreType.DMA((2, rows)),
                pltpu.SemaphoreType.DMA((2, rows)),
            ],
            compiler_params=pltpu.CompilerParams(
                collective_id=1, has_side_effects=True, vmem_limit_bytes=56 * mib
            ),
        )(sigma_anc.reshape(slots, BLK, across))
        chosen = pl.pallas_call(
            functools.partial(choose, cols),
            grid=(fronts,),
            out_shape=jax.ShapeDtypeStruct((fronts, pieces, lines, depth), kind),
            in_specs=[smem, vmem],
            out_specs=pl.BlockSpec((1, pieces, lines, depth), lambda front: (front, 0, 0, 0)),
            compiler_params=pltpu.CompilerParams(vmem_limit_bytes=56 * mib),
        )(update_blocks, dealt.reshape(2 * rows * slots, strip, across))
        result = pl.pallas_call(
            functools.partial(kernel, fronts, rows, cols),
            out_shape=jax.ShapeDtypeStruct((UB, BLK, share), kind),
            in_specs=[hbm, hbm],
            out_specs=vmem,
            scratch_shapes=[
                pltpu.VMEM((depth, wide), kind),
                pltpu.VMEM((fronts, pieces, lines, depth), kind),
                pltpu.VMEM((fronts, pieces, cols, lines, share), kind),
                pltpu.VMEM((fronts, pieces, cols - 1, lines, share), kind),
                pltpu.SemaphoreType.DMA((pieces,)),
                pltpu.SemaphoreType.DMA,
                pltpu.SemaphoreType.DMA((fronts - 1, pieces)),
                pltpu.SemaphoreType.DMA((fronts - 1, pieces)),
                pltpu.SemaphoreType.DMA((fronts, pieces, cols - 1)),
                pltpu.SemaphoreType.DMA((fronts, pieces, cols - 1)),
                pltpu.SemaphoreType.DMA((fronts, pieces, rows - 1)),
                pltpu.SemaphoreType.DMA((fronts, pieces, rows - 1)),
            ],
            compiler_params=pltpu.CompilerParams(
                collective_id=0, has_side_effects=True, vmem_limit_bytes=56 * mib
            ),
            cost_estimate=pl.CostEstimate(
                flops=2 * fronts * pieces * lines * depth * wide,
                bytes_accessed=2 * (sigma_anc.size + panel[0].size),
                transcendentals=0,
            ),
        )(chosen, panel[0])
        product = pl.pallas_call(
            functools.partial(arrange, slots, rows),
            out_shape=jax.ShapeDtypeStruct((share, UB // rows * BLK), kind),
            in_specs=[smem, vmem],
            out_specs=vmem,
            compiler_params=pltpu.CompilerParams(vmem_limit_bytes=56 * mib),
        )(update_blocks, result)
        return product[None]

    placed = (P(("front", "row"), "col"), P(), P("front", "col", None))
    return jax.shard_map(
        on_device, mesh=mesh, in_specs=placed, out_specs=P("front", "col", "row"), check_vma=False
    )
```

```python
import functools

import jax
import jax.numpy as jnp
from jax import lax
from jax.experimental import pallas as pl
from jax.experimental.pallas import tpu as pltpu
from jax.sharding import PartitionSpec as P

BLK = 128
NANC = 4
SEPB = 16
UB = 32
MESH = pl.DeviceIdType.MESH


def flipped(index, mask, count):
    total, bit = 0, 1
    while bit < count:
        digit = lax.rem(lax.div(index, bit), 2)
        total = total + (1 - digit if mask & bit else digit) * bit
        bit *= 2
    return total


def deal(fronts, rows, sigma_ref, dealt_ref, own_sem, send_sem, recv_sem):
    my_front = lax.axis_index("front")
    my_row = lax.axis_index("row")
    strip = BLK // (2 * rows)
    side = lax.rem(my_front, 2)
    place = side * rows + my_row

    def strips(to_side, to_row):
        return sigma_ref.at[:, pl.ds(pl.multiple_of((to_row * 2 + to_side) * strip, strip), strip)]

    moves = [(flip, step) for flip in (1, 0) for step in range(rows) if flip or step]

    def target(flip, step):
        return {
            "front": flipped(my_front, flip, fronts),
            "row": lax.rem(my_row + step, rows),
        }

    own = pltpu.make_async_copy(strips(side, my_row), dealt_ref.at[place], own_sem)
    own.start()
    barrier = pltpu.get_barrier_semaphore()
    for flip, step in moves:
        pl.semaphore_signal(barrier, inc=1, device_id=target(flip, step), device_id_type=MESH)
    pl.semaphore_wait(barrier, len(moves))
    copies = []
    for flip, step in moves:
        to_side = 1 - side if flip else side
        copies.append(
            pltpu.make_async_remote_copy(
                src_ref=strips(to_side, lax.rem(my_row + step, rows)),
                dst_ref=dealt_ref.at[place],
                send_sem=send_sem.at[flip, step],
                recv_sem=recv_sem.at[flip, step],
                device_id=target(flip, step),
                device_id_type=MESH,
            )
        )
    for copy in copies:
        copy.start()
    own.wait()
    for copy in copies:
        copy.wait()


def choose(cols, ids_ref, dealt_ref, chosen_ref):
    front = pl.program_id(0)
    octant = lax.div(lax.axis_index("front"), 2)
    my_col = lax.axis_index("col")
    octant_blocks = NANC * SEPB // cols
    picks = UB // cols
    pieces = chosen_ref.shape[1]
    strip = dealt_ref.shape[1]
    each = picks // pieces
    lanes = []
    for j in range(picks):
        column = ids_ref[front, my_col * picks + j] - my_col * octant_blocks
        lanes.append(pl.ds(pl.multiple_of(column * BLK, BLK), BLK))
    for p in range(picks):
        block = ids_ref[front, octant * picks + p] - octant * octant_blocks
        at = p % each * strip
        for j in range(picks):
            chosen_ref[0, p // each, at:at + strip, j * BLK:(j + 1) * BLK] = dealt_ref[block, :, lanes[j]]


def kernel(
    fronts, rows, cols,
    chosen_ref, panel_ref, result,
    panel, inbox, part, landed,
    own_sem, panel_sem, send_sem, recv_sem, part_send, part_recv, row_send, row_recv,
):
    my_front = lax.axis_index("front")
    my_row = lax.axis_index("row")
    my_col = lax.axis_index("col")
    pieces = chosen_ref.shape[1]
    strip = BLK // (2 * rows)
    picks = UB // cols
    each = picks // pieces
    wide = panel_ref.shape[1]
    share = wide // cols
    tile = min(512, share)
    per_share = share // tile
    masks = list(range(fronts - 1, 0, -1))
    order = masks[::-1]

    def own_copy(piece):
        return pltpu.make_async_copy(
            chosen_ref.at[my_front, piece], inbox.at[0, piece], own_sem.at[piece]
        )

    panel_copy = pltpu.make_async_copy(panel_ref, panel, panel_sem)

    barrier = pltpu.get_barrier_semaphore()
    for mask in masks:
        pl.semaphore_signal(
            barrier, inc=1, device_id={"front": flipped(my_front, mask, fronts)}, device_id_type=MESH
        )
    for step in range(1, cols):
        pl.semaphore_signal(
            barrier, inc=1, device_id={"col": lax.rem(my_col + step, cols)}, device_id_type=MESH
        )
    for step in range(1, rows):
        pl.semaphore_signal(
            barrier, inc=1, device_id={"row": lax.rem(my_row + step, rows)}, device_id_type=MESH
        )
    pl.semaphore_wait(barrier, fronts + cols + rows - 3)

    def front_copy(mask, piece):
        return pltpu.make_async_remote_copy(
            src_ref=chosen_ref.at[flipped(my_front, mask, fronts), piece],
            dst_ref=inbox.at[mask, piece],
            send_sem=send_sem.at[mask - 1, piece],
            recv_sem=recv_sem.at[mask - 1, piece],
            device_id={"front": flipped(my_front, mask, fronts)},
            device_id_type=MESH,
        )

    def dispatch(piece, carry):
        for mask in masks:
            front_copy(mask, piece).start()
        return carry

    lax.fori_loop(0, pieces, dispatch, 0)
    for piece in range(pieces):
        own_copy(piece).start()
    panel_copy.start()
    for piece in range(pieces):
        own_copy(piece).wait()
    panel_copy.wait()

    def part_copy(mask, piece, step):
        return pltpu.make_async_remote_copy(
            src_ref=part.at[mask, piece, lax.rem(my_col + step, cols)],
            dst_ref=landed.at[mask, piece, step - 1],
            send_sem=part_send.at[mask, piece, step - 1],
            recv_sem=part_recv.at[mask, piece, step - 1],
            device_id={"col": lax.rem(my_col + step, cols)},
            device_id_type=MESH,
        )

    def spot(mask, piece, row):
        source = flipped(my_front, mask, fronts)
        first = lax.div(source, 2) * picks + piece * each
        offset = (row * 2 + lax.rem(source, 2)) * strip
        return first, pl.ds(pl.multiple_of(offset, strip), strip)

    def row_copy(mask, piece, kind):
        first, lines = spot(mask, piece, flipped(my_row, 2, rows) if kind == 2 else my_row)
        return pltpu.make_async_remote_copy(
            src_ref=result.at[pl.ds(first, each), lines],
            dst_ref=result.at[pl.ds(first, each), lines],
            send_sem=row_send.at[mask, piece, kind],
            recv_sem=row_recv.at[mask, piece, kind],
            device_id={"row": flipped(my_row, 1 if kind else 2, rows)},
            device_id_type=MESH,
        )

    def relay(mask, piece):
        row_copy(mask, piece, 0).wait_recv()
        row_copy(mask, piece, 2).start()

    def multiply(mask, piece):
        def one_tile(n, carry):
            lanes = pl.ds(pl.multiple_of(n * tile, tile), tile)
            inner = pl.ds(pl.multiple_of(lax.rem(n, per_share) * tile, tile), tile)
            product = jnp.dot(inbox[mask, piece], panel[:, lanes], preferred_element_type=jnp.float32)
            part[mask, piece, lax.div(n, per_share), :, inner] = product.astype(part.dtype)
            return carry

        lax.fori_loop(0, wide // tile, one_tile, 0)
        for step in range(1, cols):
            part_copy(mask, piece, step).start()

    def finish(mask, piece):
        for step in range(1, cols):
            part_copy(mask, piece, step).wait_recv()
        first, lines = spot(mask, piece, my_row)
        for p in range(each):
            inside = slice(p * strip, (p + 1) * strip)
            total = part[mask, piece, my_col, inside, :].astype(jnp.float32)
            for step in range(1, cols):
                total = total + landed[mask, piece, step - 1, inside, :].astype(jnp.float32)
            result[first + p, lines, :] = (-total).astype(result.dtype)
        row_copy(mask, piece, 0).start()
        row_copy(mask, piece, 1).start()

    def own_product(piece, carry):
        multiply(0, piece)
        return carry

    def own_total(piece, carry):
        finish(0, piece)
        return carry

    lax.fori_loop(0, pieces, own_product, 0)
    lax.fori_loop(0, pieces, own_total, 0)

    def own_relay(piece, carry):
        relay(0, piece)
        return carry

    lax.fori_loop(0, pieces, own_relay, 0)

    def arrival(piece, carry):
        for at, mask in enumerate(order):
            front_copy(mask, piece).wait_recv()
            multiply(mask, piece)
            for lag, action in ((1, finish), (2, relay)):
                if at >= lag:
                    action(order[at - lag], piece)
                else:
                    @pl.when(piece > 0)
                    def _(action=action, earlier=order[at - lag]):
                        action(earlier, piece - 1)
        return carry

    lax.fori_loop(0, pieces, arrival, 0)
    finish(order[-1], pieces - 1)
    relay(order[-2], pieces - 1)
    relay(order[-1], pieces - 1)

    def drain(piece, carry):
        for mask in range(fronts):
            if mask > 0:
                front_copy(mask, piece).wait_send()
            for step in range(1, cols):
                part_copy(mask, piece, step).wait_send()
            row_copy(mask, piece, 0).wait_send()
            row_copy(mask, piece, 1).wait()
            row_copy(mask, piece, 2).wait()
        return carry

    lax.fori_loop(0, pieces, drain, 0)


def arrange(slots, rows, ids_ref, result_ref, out_ref):
    my_front = lax.axis_index("front")
    my_row = lax.axis_index("row")
    class_picks = UB // rows
    count = jnp.int32(0)
    places = [jnp.int32(0)] * class_picks
    for i in range(UB):
        hit = lax.rem(lax.div(ids_ref[my_front, i], slots), rows) == my_row
        for k in range(min(class_picks, i + 1)):
            places[k] = jnp.where(jnp.logical_and(hit, count == k), i, places[k])
        count = count + jnp.where(hit, 1, 0)
    for k, place in enumerate(places):
        out_ref[:, k * BLK:(k + 1) * BLK] = result_ref[place].T


def solution(mesh):
    fronts, rows, cols = mesh.shape["front"], mesh.shape["row"], mesh.shape["col"]

    def on_device(sigma_anc, update_blocks, panel):
        depth, wide = panel.shape[1:]
        share = wide // cols
        slots = sigma_anc.shape[0] // BLK
        across = sigma_anc.shape[1]
        kind = sigma_anc.dtype
        strip = BLK // (2 * rows)
        picks = UB // cols
        pieces = min(8, picks)
        lines = picks // pieces * strip
        smem = pl.BlockSpec(memory_space=pltpu.SMEM)
        vmem = pl.BlockSpec(memory_space=pltpu.VMEM)
        hbm = pl.BlockSpec(memory_space=pl.ANY)
        mib = 1024 * 1024
        dealt = pl.pallas_call(
            functools.partial(deal, fronts, rows),
            out_shape=jax.ShapeDtypeStruct((2 * rows, slots, strip, across), kind),
            in_specs=[hbm],
            out_specs=hbm,
            scratch_shapes=[
                pltpu.SemaphoreType.DMA,
                pltpu.SemaphoreType.DMA((2, rows)),
                pltpu.SemaphoreType.DMA((2, rows)),
            ],
            compiler_params=pltpu.CompilerParams(
                collective_id=1, has_side_effects=True, vmem_limit_bytes=56 * mib
            ),
        )(sigma_anc.reshape(slots, BLK, across))
        chosen = pl.pallas_call(
            functools.partial(choose, cols),
            grid=(fronts,),
            out_shape=jax.ShapeDtypeStruct((fronts, pieces, lines, depth), kind),
            in_specs=[smem, vmem],
            out_specs=pl.BlockSpec((1, pieces, lines, depth), lambda front: (front, 0, 0, 0)),
            compiler_params=pltpu.CompilerParams(vmem_limit_bytes=56 * mib),
        )(update_blocks, dealt.reshape(2 * rows * slots, strip, across))
        result = pl.pallas_call(
            functools.partial(kernel, fronts, rows, cols),
            out_shape=jax.ShapeDtypeStruct((UB, BLK, share), kind),
            in_specs=[hbm, hbm],
            out_specs=vmem,
            scratch_shapes=[
                pltpu.VMEM((depth, wide), kind),
                pltpu.VMEM((fronts, pieces, lines, depth), kind),
                pltpu.VMEM((fronts, pieces, cols, lines, share), kind),
                pltpu.VMEM((fronts, pieces, cols - 1, lines, share), kind),
                pltpu.SemaphoreType.DMA((pieces,)),
                pltpu.SemaphoreType.DMA,
                pltpu.SemaphoreType.DMA((fronts - 1, pieces)),
                pltpu.SemaphoreType.DMA((fronts - 1, pieces)),
                pltpu.SemaphoreType.DMA((fronts, pieces, cols - 1)),
                pltpu.SemaphoreType.DMA((fronts, pieces, cols - 1)),
                pltpu.SemaphoreType.DMA((fronts, pieces, rows - 1)),
                pltpu.SemaphoreType.DMA((fronts, pieces, rows - 1)),
            ],
            compiler_params=pltpu.CompilerParams(
                collective_id=0, has_side_effects=True, vmem_limit_bytes=56 * mib
            ),
            cost_estimate=pl.CostEstimate(
                flops=2 * fronts * pieces * lines * depth * wide,
                bytes_accessed=2 * (sigma_anc.size + panel[0].size),
                transcendentals=0,
            ),
        )(chosen, panel[0])
        product = pl.pallas_call(
            functools.partial(arrange, slots, rows),
            out_shape=jax.ShapeDtypeStruct((share, UB // rows * BLK), kind),
            in_specs=[smem, vmem],
            out_specs=vmem,
            compiler_params=pltpu.CompilerParams(vmem_limit_bytes=56 * mib),
        )(update_blocks, result)
        return product[None]

    placed = (P(("front", "row"), "col"), P(), P("front", "col", None))
    return jax.shard_map(
        on_device, mesh=mesh, in_specs=placed, out_specs=P("front", "col", "row"), check_vma=False
    )
```
